32 devices in a mesh: bins: 8 (over z, core), diag: 4 (over y, x).
Axes of the slice: x: 2, y: 2, z: 4, core: 2. Of those that a mesh axis runs over, the one named last changes fastest.
Arguments:
- embeddings: bfloat16 [1024, 512], P('bins'), may hold values from -6 to 6
- w_row: bfloat16 [512, 32], replicated, may hold values from -0.25 to 0.25
- w_col: bfloat16 [512, 32], replicated, may hold values from -0.25 to 0.25
- conv_w: bfloat16 [2, 9, 32, 32], replicated, may hold values from -0.375 to 0.375
- coef: float32 [2, 8, 32], replicated, may hold values from 0.5 to 2
- w_out: float32 [32], replicated, may hold values from -1 to 1
- dilation: int32 [2], replicated, may hold values from 1 to 32, as said below
- band_tiles: int32 [8], replicated, may hold values from 1 to 4
- bucket: int32 [4], replicated, may hold values from 0 to 7
- target: float32 [1024, 512], P('bins', 'diag'), may hold values from -6 to 6
Outputs:
- loss: float32 [1], replicated
- grad_embeddings: float32 [1024, 512], P('bins')
- grad_conv: float32 [2, 9, 32, 32], replicated
- grad_coef: float32 [2, 8, 32], replicated
- grad_out: float32 [32], replicated
- grad_row: float32 [512, 32], replicated
- grad_col: float32 [512, 32], replicated
The draws below stay inside these ranges and needn't reach their ends.
Inputs may be any that keep to these rules, and one draw needn't show every extreme that they name: Each entry is a power of two; some layer has dilation 32.
All inputs are finite; a program needn't handle non-finite values.
Results may differ from the reference program's by a relative error of at most 0.011.
Values may be sent and summed in bfloat16 or wider, within the bound.
A program may use at most 64 MiB of HBM per device.

```python
import math
import jax
import jax.numpy as jnp
from jax import lax

CHANNELS = 512
MAPS = 32
TILE = 128
LAYERS = 2
REACH = 32
BUCKETS = 8
ROWS_DEV = 128
BINS = 1024
TILE_ROWS = 8
BAND = 4
BAND_COLS = 512
N_BINS = 8
N_DIAG = 4


def draw_dilation(key, part):
    key = jax.random.fold_in(key, 11)
    first_key, second_key = jax.random.split(key)
    highest = REACH.bit_length() - 1
    powers = jax.random.randint(first_key, (LAYERS,), 0, highest + 1)
    chosen = jax.random.randint(second_key, (), 0, LAYERS)
    powers = jnp.where(jnp.arange(LAYERS) == chosen, highest, powers).astype(jnp.int32)
    return jnp.left_shift(jnp.ones((LAYERS,), jnp.int32), powers)


def place_ends(result, key, least, high):
    dims = result.shape
    spot = [jax.random.randint(jax.random.fold_in(key, axis), (), 0, dims[axis]) for axis in range(len(dims))]
    result = result.at[tuple(spot)].set(least)
    longest = dims.index(max(dims))
    spot[longest] = (spot[longest] + 1) % dims[longest]
    return result.at[tuple(spot)].set(high)


def level_of(key, dims, pieces, smallest, high):
    loudness, own = 1.0, jax.random.fold_in(key, 6)
    for position, blocks in pieces:
        draws = jnp.exp(jax.random.uniform(jax.random.fold_in(own, position), (blocks,), jnp.float32, smallest / len(pieces), high / len(pieces)))
        loudness = loudness * jnp.repeat(draws, dims[position] // blocks).reshape([-1 if axis == position else 1 for axis in range(len(dims))])
    return loudness


def gaussian(stream_key, shape, scale, reach, cuts=(), kind=jnp.bfloat16):
    values = scale * jax.random.normal(stream_key, shape, jnp.float32)
    if cuts:
        values = values * level_of(stream_key, shape, cuts, -0.22, 0.18)
    return jnp.clip(values, -reach, reach).astype(kind)


def setup_inputs(seed: int = 0) -> dict:
    seeds = jax.random.split(jax.random.key(seed), 11)
    return {
        "embeddings": gaussian(seeds[0], (BINS, CHANNELS), 1.0, 6.0, ((0, 8),)),
        "w_row": gaussian(seeds[1], (CHANNELS, MAPS), CHANNELS ** -0.5, 0.25),
        "w_col": gaussian(seeds[2], (CHANNELS, MAPS), CHANNELS ** -0.5, 0.25),
        "conv_w": gaussian(seeds[3], (LAYERS, 9, MAPS, MAPS), (9 * MAPS) ** -0.5, 0.375),
        "coef": jnp.clip(jnp.exp(jax.random.uniform(seeds[4], (LAYERS, BUCKETS, MAPS), jnp.float32, math.log(0.5), math.log(2.0))), 0.5, 2.0),
        "w_out": gaussian(seeds[5], (MAPS,), MAPS ** -0.5, 1.0, (), jnp.float32),
        "dilation": draw_dilation(jax.random.fold_in(seeds[10], 71), 0),
        "band_tiles": place_ends(jax.random.randint(seeds[7], (TILE_ROWS,), 1, BAND + 1), jax.random.fold_in(seeds[7], 1), 1, BAND).astype(jnp.int32),
        "bucket": place_ends(jax.random.randint(seeds[8], (BAND,), 0, BUCKETS), jax.random.fold_in(seeds[8], 1), 0, BUCKETS - 1).astype(jnp.int32),
        "target": gaussian(seeds[9], (BINS, BAND_COLS), 1.0, 6.0, ((0, 8), (1, 4)), jnp.float32),
    }


def skew_take(vector, rows, width):
    length = rows + width
    maps = vector.shape[0]
    spread = jnp.broadcast_to(vector[:, None, :length], (maps, rows, length))
    flat = jnp.pad(spread.reshape(maps, rows * length), ((0, 0), (0, rows)))
    return flat.reshape(maps, rows, length + 1)[:, :, :width]

def skew_back(vector, rows, width):
    flipped = jnp.pad(vector[:, ::-1], ((0, 0), (0, 1)))
    return skew_take(flipped, rows, width)[:, ::-1, :]

def skew_sum(field):
    maps, rows, width = field.shape
    length = rows + width
    padded = jnp.pad(field, ((0, 0), (0, 0), (0, rows)))
    flat = padded.reshape(maps, rows * length)[:, :rows * (length - 1)]
    return lax.optimization_barrier(jnp.sum(flat.reshape(maps, rows, length - 1), axis=1))

def sum_back(field):
    return skew_sum(field[:, ::-1, :])[:, ::-1]

def convolve(padded, weights, dilate, rows, width):
    anchor = jnp.zeros((), jnp.int32)
    total = jnp.zeros((weights.shape[1], rows, width), jnp.float32)
    for place in range(9):
        down = REACH + (place // 3 - 1) * dilate
        right = REACH + (place % 3 - 1) * dilate
        window = lax.dynamic_slice(padded, (anchor, down, right), (padded.shape[0], rows, width))
        total = total + jnp.einsum('ok,kxs->oxs', weights[place].astype(jnp.float32), window.astype(jnp.float32))
    return total

def convolve_back(padded, weights, dilate, rows, width):
    anchor = jnp.zeros((), jnp.int32)
    total = jnp.zeros((weights.shape[2], rows, width), jnp.float32)
    for place in range(9):
        down = REACH - (place // 3 - 1) * dilate
        right = REACH - (place % 3 - 1) * dilate
        window = lax.dynamic_slice(padded, (anchor, down, right), (padded.shape[0], rows, width))
        total = total + jnp.einsum('ok,oxs->kxs', weights[place].astype(jnp.float32), window.astype(jnp.float32))
    return total

def kernel_grad(grad_mixed, padded, dilate, rows, width):
    anchor = jnp.zeros((), jnp.int32)
    parts = []
    for place in range(9):
        down = REACH + (place // 3 - 1) * dilate
        right = REACH + (place % 3 - 1) * dilate
        window = lax.dynamic_slice(padded, (anchor, down, right), (padded.shape[0], rows, width))
        parts.append(jnp.einsum('oxs,kxs->ok', grad_mixed.astype(jnp.float32), window.astype(jnp.float32)))
    return jnp.stack(parts)

def reference(embeddings, w_row, w_col, conv_w, coef, w_out, dilation, band_tiles, bucket, target):
    margin = LAYERS * REACH
    ext_rows = ROWS_DEV + 2 * margin
    total_bins = ROWS_DEV * N_BINS
    band_cols = TILE * N_DIAG
    tile_total = band_tiles.shape[0]
    row_proj = jnp.dot(embeddings, w_row, preferred_element_type=jnp.float32).astype(jnp.bfloat16)
    col_proj = jnp.dot(embeddings, w_col, preferred_element_type=jnp.float32).astype(jnp.bfloat16)
    row_table = jnp.pad(row_proj.T, ((0, 0), (margin, margin)))
    column_table = jnp.pad(col_proj.T, ((0, 0), (margin + band_cols, margin)))
    target_table = jnp.pad(target, ((margin, margin), (0, 0)))
    choose = (bucket[:, None] == jnp.arange(BUCKETS, dtype=jnp.int32)[None, :]).astype(jnp.float32)
    column_scale = jnp.transpose(jnp.repeat(coef[:, bucket, :], TILE, axis=1), (0, 2, 1))
    zero = jnp.zeros((), jnp.int32)
    positions = jnp.arange(ext_rows, dtype=jnp.int32)
    offsets = jnp.arange(band_cols, dtype=jnp.int32)[None, :]
    core = ((positions >= margin) & (positions < margin + ROWS_DEV)).astype(jnp.float32)[:, None]

    def block(carry, index):
        row_acc, col_acc, kernels, coef_acc, out_acc, loss_acc = carry
        start = (index * ROWS_DEV).astype(jnp.int32)
        row_part = lax.dynamic_slice(row_table, (zero, start), (MAPS, ext_rows))
        vector = lax.dynamic_slice(column_table, (zero, start + 1), (MAPS, ext_rows + band_cols - 1))
        sheared = skew_back(vector, ext_rows, band_cols)
        bins_here = (start - margin + positions)[:, None]
        tile_index = jnp.clip(bins_here // TILE, 0, tile_total - 1).astype(jnp.int32)
        row_limit = band_tiles[tile_index] * TILE
        mask = ((bins_here >= 0) & (bins_here < total_bins) & (offsets < row_limit) & (bins_here - offsets >= 0)).astype(jnp.float32)
        preact = row_part.astype(jnp.float32)[:, :, None] + sheared.astype(jnp.float32)
        state = (mask * jax.nn.silu(preact)).astype(jnp.bfloat16)
        pads = []
        values = []
        for layer in range(LAYERS):
            padded = jnp.pad(state, ((0, 0), (REACH, REACH), (REACH, REACH)))
            mixed = convolve(padded, conv_w[layer], dilation[layer], ext_rows, band_cols)
            pads.append(padded)
            values.append(mixed)
            state = (mask * (state.astype(jnp.float32) + column_scale[layer][:, None, :] * jax.nn.silu(mixed))).astype(jnp.bfloat16)
        pred = mask * lax.optimization_barrier(jnp.sum(w_out[:, None, None] * state.astype(jnp.float32), axis=0))
        goal = lax.dynamic_slice(target_table, (start, zero), (ext_rows, band_cols))
        weight = mask * core
        resid = weight * (pred - goal)
        loss_acc = loss_acc + 0.5 * jnp.sum(resid * resid)
        out_acc = out_acc + lax.optimization_barrier(jnp.sum(resid[None] * state.astype(jnp.float32), axis=(1, 2)))
        adjoint = w_out[:, None, None] * resid[None]
        for layer in reversed(range(LAYERS)):
            mixed = values[layer]
            gate = jax.nn.sigmoid(mixed)
            slope = gate * (1.0 + mixed * (1.0 - gate))
            per_column = lax.optimization_barrier(jnp.sum(adjoint * jax.nn.silu(mixed), axis=1))
            per_diag = lax.optimization_barrier(jnp.sum(per_column.reshape(MAPS, N_DIAG, TILE), axis=2))
            coef_acc = coef_acc.at[layer].add(jnp.dot(per_diag, choose, precision=lax.Precision.HIGHEST).T)
            grad_mixed = (adjoint * column_scale[layer][:, None, :] * slope).astype(jnp.bfloat16)
            kernels = kernels.at[layer].add(kernel_grad(grad_mixed, pads[layer], dilation[layer], ext_rows, band_cols))
            grad_pad = jnp.pad(grad_mixed, ((0, 0), (REACH, REACH), (REACH, REACH)))
            adjoint = mask * (adjoint + convolve_back(grad_pad, conv_w[layer], dilation[layer], ext_rows, band_cols))
        gate = jax.nn.sigmoid(preact)
        grad_pre = adjoint * gate * (1.0 + preact * (1.0 - gate))
        row_old = lax.dynamic_slice(row_acc, (zero, start), (MAPS, ext_rows))
        row_acc = lax.dynamic_update_slice(row_acc, row_old + lax.optimization_barrier(jnp.sum(grad_pre, axis=2)), (zero, start))
        span = ext_rows + band_cols - 1
        col_old = lax.dynamic_slice(col_acc, (zero, start + 1), (MAPS, span))
        col_acc = lax.dynamic_update_slice(col_acc, col_old + sum_back(grad_pre), (zero, start + 1))
        return ((row_acc, col_acc, kernels, coef_acc, out_acc, loss_acc), None)
    init = (jnp.zeros((MAPS, total_bins + 2 * margin), jnp.float32), jnp.zeros((MAPS, total_bins + 2 * margin + band_cols), jnp.float32), jnp.zeros((LAYERS, 9, MAPS, MAPS), jnp.float32), jnp.zeros((LAYERS, BUCKETS, MAPS), jnp.float32), jnp.zeros((MAPS,), jnp.float32), jnp.zeros((), jnp.float32))
    carry, _ = lax.scan(block, init, jnp.arange(N_BINS, dtype=jnp.int32))
    row_acc, col_acc, kernels, coef_acc, out_acc, loss_acc = carry
    row_grad = row_acc[:, margin:margin + total_bins].T.astype(jnp.bfloat16)
    col_grad = col_acc[:, margin + band_cols:margin + band_cols + total_bins].T.astype(jnp.bfloat16)
    grad_embeddings = jnp.dot(row_grad, w_row.T, preferred_element_type=jnp.float32) + jnp.dot(col_grad, w_col.T, preferred_element_type=jnp.float32)
    all_bins = jnp.arange(total_bins, dtype=jnp.int32)
    all_limit = band_tiles[(all_bins // TILE).astype(jnp.int32)] * TILE
    count = jnp.sum(jnp.minimum(all_limit, all_bins + 1)).astype(jnp.float32)
    inv_root = 1.0 / jnp.sqrt(count)
    grad_row = jnp.dot(embeddings.T, row_grad, preferred_element_type=jnp.float32) * inv_root
    grad_col = jnp.dot(embeddings.T, col_grad, preferred_element_type=jnp.float32) * inv_root
    loss = jnp.reshape(loss_acc / count, (1,))
    return (loss, grad_embeddings, kernels * inv_root, coef_acc * inv_root, out_acc * inv_root, grad_row, grad_col)
```

```python
import jax
import jax.numpy as jnp
from jax import lax
from jax.experimental import pallas as pl
from jax.experimental.pallas import tpu as pltpu
from jax.sharding import PartitionSpec as P

MAPS = 32
TILE = 128
LAYERS = 2
REACH = 32
BUCKETS = 8


MESH = pl.DeviceIdType.MESH


def reduce_kernel(nb, nd, x_ref, o_ref, buf_a, acc_a, buf_b, acc_b, *sems):
    sa, ra, sb, rb, sc, rc, sd, rd = sems
    b = lax.axis_index("bins")
    g = lax.axis_index("diag")
    rows_a = x_ref.shape[0] // nd
    rows_b = rows_a // nb
    peers_g = [lax.rem(g + k, nd) for k in range(nd)]
    peers_b = [lax.rem(b + k, nb) for k in range(nb)]
    barrier = pltpu.get_barrier_semaphore()
    for k in range(1, nd):
        pl.semaphore_signal(barrier, inc=1, device_id=(b, peers_g[k]), device_id_type=MESH)
    for k in range(1, nb):
        pl.semaphore_signal(barrier, inc=1, device_id=(peers_b[k], g), device_id_type=MESH)
    pl.semaphore_wait(barrier, nd + nb - 2)

    def rows_of(index, count):
        return pl.ds(pl.multiple_of(index * count, 8), count)

    def send(src, dst, ssem, rsem, target):
        copy = pltpu.make_async_remote_copy(
            src_ref=src,
            dst_ref=dst,
            send_sem=ssem,
            recv_sem=rsem,
            device_id=target,
            device_id_type=MESH,
        )
        copy.start()
        return copy

    copies = [
        send(
            x_ref.at[rows_of(peers_g[k], rows_a)],
            buf_a.at[k],
            sa.at[k],
            ra.at[k],
            (b, peers_g[k]),
        )
        for k in range(1, nd)
    ]
    total = x_ref[rows_of(g, rows_a), :]
    for k in range(1, nd):
        copies[k - 1].wait()
        total = total + buf_a[k]
    acc_a[...] = total
    copies = [
        send(
            acc_a.at[rows_of(peers_b[k], rows_b)],
            buf_b.at[k],
            sb.at[k],
            rb.at[k],
            (peers_b[k], g),
        )
        for k in range(1, nb)
    ]
    total = acc_a[rows_of(b, rows_b), :]
    for k in range(1, nb):
        copies[k - 1].wait()
        total = total + buf_b[k]
    acc_b[rows_of(b, rows_b), :] = total
    mine = acc_b.at[rows_of(b, rows_b)]
    copies = [
        send(mine, mine, sc.at[k], rc.at[k], (peers_b[k], g)) for k in range(1, nb)
    ]
    for copy in copies:
        copy.wait()
    o_ref[rows_of(g, rows_a), :] = acc_b[...]
    place = o_ref.at[rows_of(g, rows_a)]
    copies = [
        send(acc_b, place, sd.at[k], rd.at[k], (b, peers_g[k])) for k in range(1, nd)
    ]
    for copy in copies:
        copy.wait()


def all_sum(flat, ident):
    nb, nd = lax.axis_size("bins"), lax.axis_size("diag")
    unit = nb * nd * 8
    rows = -(-flat.shape[0] // (128 * unit)) * unit
    x = jnp.pad(flat, (0, rows * 128 - flat.shape[0])).reshape(rows, 128)
    rows_a, rows_b = rows // nd, rows // nd // nb
    dma = pltpu.SemaphoreType.DMA
    out = pl.pallas_call(
        lambda *refs: reduce_kernel(nb, nd, *refs),
        out_shape=jax.ShapeDtypeStruct((rows, 128), jnp.float32),
        in_specs=[pl.BlockSpec(memory_space=pltpu.VMEM)],
        out_specs=pl.BlockSpec(memory_space=pltpu.VMEM),
        scratch_shapes=[
            pltpu.VMEM((nd, rows_a, 128), jnp.float32),
            pltpu.VMEM((rows_a, 128), jnp.float32),
            pltpu.VMEM((nb, rows_b, 128), jnp.float32),
            pltpu.VMEM((rows_a, 128), jnp.float32),
            dma((nd,)),
            dma((nd,)),
            dma((nb,)),
            dma((nb,)),
            dma((nb,)),
            dma((nb,)),
            dma((nd,)),
            dma((nd,)),
        ],
        compiler_params=pltpu.CompilerParams(
            collective_id=ident, has_side_effects=True, vmem_limit_bytes=16 * 2**20
        ),
    )(x)
    return out.reshape(-1)[: flat.shape[0]]


def extended(cells, sides, width):
    for axis, dim in sides:
        count = lax.axis_size(axis)
        ends = count - 1
        head = lax.slice_in_dim(cells, 0, width, axis=dim)
        tail = lax.slice_in_dim(cells, cells.shape[dim] - width, cells.shape[dim], axis=dim)
        cells = jnp.concatenate(
            [
                lax.ppermute(tail, axis, [(i, (i + 1) % count) for i in range(ends)]),
                cells,
                lax.ppermute(head, axis, [((i + 1) % count, i) for i in range(ends)]),
            ],
            axis=dim,
        )
    return cells


def skew_take(vector, rows, width):
    length = rows + width
    maps = vector.shape[0]
    spread = jnp.broadcast_to(vector[:, None, :length], (maps, rows, length))
    flat = jnp.pad(spread.reshape(maps, rows * length), ((0, 0), (0, rows)))
    return flat.reshape(maps, rows, length + 1)[:, :, :width]


def skew_back(vector, rows, width):
    flipped = jnp.pad(vector[:, ::-1], ((0, 0), (0, 1)))
    return skew_take(flipped, rows, width)[:, ::-1, :]


def skew_sum(field):
    maps, rows, width = field.shape
    length = rows + width
    padded = jnp.pad(field, ((0, 0), (0, 0), (0, rows)))
    flat = padded.reshape(maps, rows * length)[:, : rows * (length - 1)]
    return jnp.sum(flat.reshape(maps, rows, length - 1), axis=1)


def sum_back(field):
    return skew_sum(field[:, ::-1, :])[:, ::-1]


def convolve(padded, weights, dilate, rows, width):
    anchor = jnp.zeros((), jnp.int32)
    total = jnp.zeros((weights.shape[1], rows, width), jnp.float32)
    for place in range(9):
        down = REACH + (place // 3 - 1) * dilate
        right = REACH + (place % 3 - 1) * dilate
        window = lax.dynamic_slice(padded, (anchor, down, right), (padded.shape[0], rows, width))
        total = total + jnp.einsum(
            "ok,kxs->oxs", weights[place], window, preferred_element_type=jnp.float32
        )
    return total


def convolve_back(padded, weights, dilate, rows, width):
    anchor = jnp.zeros((), jnp.int32)
    total = jnp.zeros((weights.shape[2], rows, width), jnp.float32)
    for place in range(9):
        down = REACH - (place // 3 - 1) * dilate
        right = REACH - (place % 3 - 1) * dilate
        window = lax.dynamic_slice(padded, (anchor, down, right), (padded.shape[0], rows, width))
        total = total + jnp.einsum(
            "ok,oxs->kxs", weights[place], window, preferred_element_type=jnp.float32
        )
    return total


def kernel_grad(grad_mixed, padded, dilate, rows, width):
    anchor = jnp.zeros((), jnp.int32)
    parts = []
    for place in range(9):
        down = REACH + (place // 3 - 1) * dilate
        right = REACH + (place % 3 - 1) * dilate
        window = lax.dynamic_slice(padded, (anchor, down, right), (padded.shape[0], rows, width))
        parts.append(
            jnp.einsum("oxs,kxs->ok", grad_mixed, window, preferred_element_type=jnp.float32)
        )
    return jnp.stack(parts)


def local(embeddings, w_row, w_col, conv_w, coef, w_out, dilation, band_tiles, bucket, target):
    rows = embeddings.shape[0]
    width = target.shape[1]
    diag_count = lax.axis_size("diag")
    total_bins = rows * lax.axis_size("bins")
    band_cols = width * diag_count
    tile_total = band_tiles.shape[0]
    zero = jnp.zeros((), jnp.int32)
    row_start = lax.axis_index("bins") * rows
    col_start = lax.axis_index("diag") * width
    device_bucket = jnp.sum(
        jnp.where(jnp.arange(diag_count, dtype=jnp.int32) == lax.axis_index("diag"), bucket, 0)
    )
    choose = (jnp.arange(BUCKETS, dtype=jnp.int32) == device_bucket).astype(jnp.float32)
    tile_ids = jnp.arange(tile_total, dtype=jnp.int32)[None, :]

    def row_limit(bins_col):
        tiles = jnp.clip(bins_col // TILE, 0, tile_total - 1)
        hits = tiles == tile_ids
        return jnp.sum(jnp.where(hits, band_tiles[None, :], 0), axis=1, keepdims=True) * TILE

    row_proj = jnp.dot(embeddings, w_row, preferred_element_type=jnp.float32).astype(jnp.bfloat16)
    col_proj = jnp.dot(embeddings, w_col, preferred_element_type=jnp.float32).astype(jnp.bfloat16)
    gathered = lax.all_gather(col_proj, "bins", axis=0, tiled=True)
    column_table = jnp.pad(gathered.T, ((0, 0), (band_cols + 2 * REACH, 2 * REACH)))
    table_base = row_start - col_start - width + 1 + band_cols
    vector = lax.dynamic_slice_in_dim(column_table, table_base + 2 * REACH, rows + width - 1, 1)
    sheared = skew_back(vector, rows, width)
    bins_here = row_start + jnp.arange(rows, dtype=jnp.int32)[:, None]
    offsets = col_start + jnp.arange(width, dtype=jnp.int32)[None, :]
    inside = (
        (bins_here >= 0)
        & (bins_here < total_bins)
        & (offsets >= 0)
        & (offsets < row_limit(bins_here))
        & (bins_here - offsets >= 0)
    )
    mask = inside.astype(jnp.float32)
    preact = row_proj.T.astype(jnp.float32)[:, :, None] + sheared.astype(jnp.float32)
    state = (mask * jax.nn.silu(preact)).astype(jnp.bfloat16)
    pads = []
    values = []
    scales = []
    for layer in range(LAYERS):
        padded = extended(state, (("bins", 1), ("diag", 2)), REACH)
        mixed = convolve(padded, conv_w[layer], dilation[layer], rows, width)
        scale = jnp.sum(choose[:, None] * coef[layer], axis=0)
        pads.append(padded)
        values.append(mixed)
        scales.append(scale)
        state = (
            mask * (state.astype(jnp.float32) + scale[:, None, None] * jax.nn.silu(mixed))
        ).astype(jnp.bfloat16)
    pred = mask * jnp.sum(w_out[:, None, None] * state.astype(jnp.float32), axis=0)
    resid = mask * (pred - target)
    loss_part = 0.5 * jnp.sum(resid * resid)
    out_grad = jnp.sum(resid[None] * state.astype(jnp.float32), axis=(1, 2))
    adjoint = w_out[:, None, None] * resid[None]
    kernels = [None] * LAYERS
    coef_terms = [None] * LAYERS
    for layer in reversed(range(LAYERS)):
        mixed = values[layer]
        gate = jax.nn.sigmoid(mixed)
        slope = gate * (1.0 + mixed * (1.0 - gate))
        coef_terms[layer] = (
            choose[:, None] * jnp.sum(adjoint * jax.nn.silu(mixed), axis=(1, 2))[None, :]
        )
        grad_mixed = (adjoint * scales[layer][:, None, None] * slope).astype(jnp.bfloat16)
        kernels[layer] = kernel_grad(grad_mixed, pads[layer], dilation[layer], rows, width)
        grad_pad = extended(grad_mixed, (("bins", 1), ("diag", 2)), REACH)
        adjoint = mask * (
            adjoint + convolve_back(grad_pad, conv_w[layer], dilation[layer], rows, width)
        )
    gate = jax.nn.sigmoid(preact)
    grad_pre = adjoint * gate * (1.0 + preact * (1.0 - gate))
    row_terms = jnp.sum(grad_pre, axis=2).T
    col_terms = sum_back(grad_pre).T
    column_full = jnp.zeros((total_bins + band_cols, MAPS), jnp.float32)
    column_full = lax.dynamic_update_slice(column_full, col_terms, (table_base, zero))
    row_full = jnp.zeros((total_bins, MAPS), jnp.float32)
    row_full = lax.dynamic_update_slice(row_full, row_terms, (row_start, zero))
    both = jnp.concatenate([row_full, column_full[band_cols:]], axis=0).reshape(-1)
    both = all_sum(both, 1).reshape(2, total_bins, MAPS)
    row_total = lax.dynamic_slice_in_dim(both[0], row_start, rows, 0)
    column_total = lax.dynamic_slice_in_dim(both[1], row_start, rows, 0)
    row_all = row_total.astype(jnp.bfloat16)
    column_all = column_total.astype(jnp.bfloat16)
    grad_embeddings = jnp.dot(row_all, w_row.T, preferred_element_type=jnp.float32) + jnp.dot(
        column_all, w_col.T, preferred_element_type=jnp.float32
    )
    share_rows = rows // diag_count
    share_start = lax.axis_index("diag") * share_rows
    row_grad = lax.dynamic_slice_in_dim(row_all, share_start, share_rows, 0)
    col_grad = lax.dynamic_slice_in_dim(column_all, share_start, share_rows, 0)
    piece_rows = lax.dynamic_slice_in_dim(embeddings, share_start, share_rows, 0)
    row_weight = jnp.dot(piece_rows.T, row_grad, preferred_element_type=jnp.float32)
    col_weight = jnp.dot(piece_rows.T, col_grad, preferred_element_type=jnp.float32)
    pieces = (
        jnp.stack(kernels),
        row_weight,
        col_weight,
        jnp.stack(coef_terms),
        out_grad,
        loss_part.reshape(1),
    )
    flat = all_sum(jnp.concatenate([p.reshape(-1) for p in pieces]), 2)
    sums = []
    at = 0
    for piece in pieces:
        sums.append(flat[at : at + piece.size].reshape(piece.shape))
        at += piece.size
    totals = (sums[5][0], sums[4], sums[0], sums[3], sums[1], sums[2])
    all_bins = jnp.arange(total_bins, dtype=jnp.int32)[:, None]
    count = jnp.sum(jnp.minimum(row_limit(all_bins)[:, 0], all_bins[:, 0] + 1)).astype(jnp.float32)
    inv_root = 1.0 / jnp.sqrt(count)
    loss = jnp.reshape(totals[0] / count, (1,))
    return (
        loss,
        grad_embeddings,
        totals[2] * inv_root,
        totals[3] * inv_root,
        totals[1] * inv_root,
        totals[4] * inv_root,
        totals[5] * inv_root,
    )


def solution(mesh):
    in_specs = (P("bins", None), P(), P(), P(), P(), P(), P(), P(), P(), P("bins", "diag"))
    out_specs = (P(), P("bins", None), P(), P(), P(), P(), P())
    return jax.shard_map(local, mesh=mesh, in_specs=in_specs, out_specs=out_specs, check_vma=False)
```

```python
import jax
import jax.numpy as jnp
from jax import lax
from jax.experimental import pallas as pl
from jax.experimental.pallas import tpu as pltpu
from jax.sharding import PartitionSpec as P

MAPS = 32
TILE = 128
LAYERS = 2
REACH = 32
BUCKETS = 8


MESH = pl.DeviceIdType.MESH


def reduce_kernel(nb, nd, x_ref, o_ref, buf_a, acc_a, buf_b, acc_b, *sems):
    sa, ra, sb, rb, sc, rc, sd, rd = sems
    b = lax.axis_index("bins")
    g = lax.axis_index("diag")
    rows_a = x_ref.shape[0] // nd
    rows_b = rows_a // nb
    peers_g = [lax.rem(g + k, nd) for k in range(nd)]
    peers_b = [lax.rem(b + k, nb) for k in range(nb)]
    barrier = pltpu.get_barrier_semaphore()
    for k in range(1, nd):
        pl.semaphore_signal(barrier, inc=1, device_id=(b, peers_g[k]), device_id_type=MESH)
    for k in range(1, nb):
        pl.semaphore_signal(barrier, inc=1, device_id=(peers_b[k], g), device_id_type=MESH)
    pl.semaphore_wait(barrier, nd + nb - 2)

    def rows_of(index, count):
        return pl.ds(pl.multiple_of(index * count, 8), count)

    def send(src, dst, ssem, rsem, target):
        copy = pltpu.make_async_remote_copy(
            src_ref=src,
            dst_ref=dst,
            send_sem=ssem,
            recv_sem=rsem,
            device_id=target,
            device_id_type=MESH,
        )
        copy.start()
        return copy

    copies = [
        send(
            x_ref.at[rows_of(peers_g[k], rows_a)],
            buf_a.at[k],
            sa.at[k],
            ra.at[k],
            (b, peers_g[k]),
        )
        for k in range(1, nd)
    ]
    total = x_ref[rows_of(g, rows_a), :]
    for k in range(1, nd):
        copies[k - 1].wait()
        total = total + buf_a[k]
    acc_a[...] = total
    copies = [
        send(
            acc_a.at[rows_of(peers_b[k], rows_b)],
            buf_b.at[k],
            sb.at[k],
            rb.at[k],
            (peers_b[k], g),
        )
        for k in range(1, nb)
    ]
    total = acc_a[rows_of(b, rows_b), :]
    for k in range(1, nb):
        copies[k - 1].wait()
        total = total + buf_b[k]
    acc_b[rows_of(b, rows_b), :] = total
    mine = acc_b.at[rows_of(b, rows_b)]
    copies = [
        send(mine, mine, sc.at[k], rc.at[k], (peers_b[k], g)) for k in range(1, nb)
    ]
    for copy in copies:
        copy.wait()
    o_ref[rows_of(g, rows_a), :] = acc_b[...]
    place = o_ref.at[rows_of(g, rows_a)]
    copies = [
        send(acc_b, place, sd.at[k], rd.at[k], (b, peers_g[k])) for k in range(1, nd)
    ]
    for copy in copies:
        copy.wait()


def all_sum(flat, ident):
    nb, nd = lax.axis_size("bins"), lax.axis_size("diag")
    unit = nb * nd * 8
    rows = -(-flat.shape[0] // (128 * unit)) * unit
    x = jnp.pad(flat, (0, rows * 128 - flat.shape[0])).reshape(rows, 128)
    rows_a, rows_b = rows // nd, rows // nd // nb
    dma = pltpu.SemaphoreType.DMA
    out = pl.pallas_call(
        lambda *refs: reduce_kernel(nb, nd, *refs),
        out_shape=jax.ShapeDtypeStruct((rows, 128), jnp.float32),
        in_specs=[pl.BlockSpec(memory_space=pltpu.VMEM)],
        out_specs=pl.BlockSpec(memory_space=pltpu.VMEM),
        scratch_shapes=[
            pltpu.VMEM((nd, rows_a, 128), jnp.float32),
            pltpu.VMEM((rows_a, 128), jnp.float32),
            pltpu.VMEM((nb, rows_b, 128), jnp.float32),
            pltpu.VMEM((rows_a, 128), jnp.float32),
            dma((nd,)),
            dma((nd,)),
            dma((nb,)),
            dma((nb,)),
            dma((nb,)),
            dma((nb,)),
            dma((nd,)),
            dma((nd,)),
        ],
        compiler_params=pltpu.CompilerParams(
            collective_id=ident, has_side_effects=True, vmem_limit_bytes=16 * 2**20
        ),
    )(x)
    return out.reshape(-1)[: flat.shape[0]]


DIRS = [(-1, 0), (1, 0), (0, -1), (0, 1), (-1, -1), (-1, 1), (1, -1), (1, 1)]
BLOCKS = 4
SUB = 32
LANES = BLOCKS * MAPS
FACE = SUB * 32
CORNER = SUB * 8


def gate_of(v):
    return 1.0 / (1.0 + jnp.exp(-v))


def rounded(v):
    return v.astype(jnp.bfloat16).astype(jnp.float32)


def lane_group(shape):
    return lax.broadcasted_iota(jnp.int32, shape, len(shape) - 1) // MAPS


def packed(cells, group):
    piece = cells.shape[1] // BLOCKS
    total = None
    for q in range(BLOCKS):
        part = cells[:, q * piece : (q + 1) * piece, :].reshape(-1, LANES)
        turn = (MAPS * (q - group)) % LANES
        part = pltpu.roll(part, turn, 1) if turn else part
        total = part if total is None else jnp.where(lane_group(part.shape) == q, part, total)
    return total


def unpacked(part, group):
    pieces = []
    for q in range(BLOCKS):
        turn = (MAPS * (group - q)) % LANES
        pieces.append(pltpu.roll(part, turn, 1) if turn else part)
    return pieces


def step_kernel(
    nb,
    nd,
    dil_ref,
    lim_ref,
    colm_ref,
    cols_ref,
    rowm_ref,
    rows_ref,
    wf_ref,
    wb_ref,
    par_ref,
    target_ref,
    kern_ref,
    stat_ref,
    rowg_ref,
    colg_ref,
    ext,
    sh0,
    sh1,
    sh2,
    cur,
    mask_buf,
    mixed_buf,
    adj_buf,
    gm_buf,
    send_face,
    send_corner,
    recv_face,
    recv_corner,
    corner_f,
    send_sem,
    recv_sem,
):
    b = lax.axis_index("bins")
    g = lax.axis_index("diag")
    row_start = b * TILE
    col_start = g * TILE

    def there(sx, sg):
        x, y = b + sx, g + sg
        return (x >= 0) & (x < nb) & (y >= 0) & (y < nd)

    def place(sx, sg):
        return (lax.rem(b + sx + nb, nb), lax.rem(g + sg + nd, nd))

    for n, (sx, sg) in enumerate(DIRS):

        @pl.when(jnp.logical_not(there(-sx, -sg)))
        def _():
            for e in range(3):
                if n < 4:
                    recv_face[e, n] = jnp.zeros((FACE, LANES), jnp.bfloat16)
                else:
                    recv_corner[e, n - 4] = jnp.zeros((CORNER, LANES), jnp.bfloat16)

    barrier = pltpu.get_barrier_semaphore()
    for sx, sg in DIRS:

        @pl.when(there(sx, sg))
        def _():
            pl.semaphore_signal(barrier, inc=1, device_id=place(sx, sg), device_id_type=MESH)

    pl.semaphore_wait(barrier, sum(there(sx, sg).astype(jnp.int32) for sx, sg in DIRS))

    def copy_of(e, n):
        if n < 4:
            src, dst = send_face.at[n], recv_face.at[e, n]
        else:
            src, dst = send_corner.at[n - 4], recv_corner.at[e, n - 4]
        return pltpu.make_async_remote_copy(
            src_ref=src,
            dst_ref=dst,
            send_sem=send_sem.at[e, n],
            recv_sem=recv_sem.at[e, n],
            device_id=place(*DIRS[n]),
            device_id_type=MESH,
        )

    def exchange_start(e):
        for n in (2, 3, 0, 1, 4, 5, 6, 7):
            sx, sg = DIRS[n]
            lo = 0 if sg < 0 else TILE - 32
            if n < 2:
                value = packed(cur[...], 0 if sx < 0 else BLOCKS - 1)
                send_face[n] = value.astype(jnp.bfloat16)
            elif n < 4:
                value = cur[:, lo : lo + 32, :].reshape(FACE, LANES)
                send_face[n] = value.astype(jnp.bfloat16)
            else:
                value = packed(cur[:, lo : lo + 32, :], 0 if sx < 0 else BLOCKS - 1)
                send_corner[n - 4] = value.astype(jnp.bfloat16)

            @pl.when(there(sx, sg))
            def _():
                copy_of(e, n).start()

    def exchange_end(e):
        for n, (sx, sg) in enumerate(DIRS):

            @pl.when(there(-sx, -sg))
            def _():
                copy_of(e, n).wait_recv()

            @pl.when(there(sx, sg))
            def _():
                copy_of(e, n).wait_send()

        for c in range(4):
            corner_f[c] = recv_corner[e, c].astype(jnp.float32)

        def fill(xi, carry):
            face_rows = pl.ds(pl.multiple_of(xi * 32, 32), 32)
            corner_rows = pl.ds(pl.multiple_of(xi * 8, 8), 8)

            def face(n):
                return recv_face[e, n, face_rows, :].astype(jnp.float32)

            def corner(n):
                return corner_f[n - 4, corner_rows, :]

            mid = jnp.concatenate([face(3), cur[xi], face(2)], axis=0)
            low = jnp.concatenate(
                unpacked(corner(7), 0) + unpacked(face(1), 0) + unpacked(corner(6), 0), axis=0
            )
            high = jnp.concatenate(
                unpacked(corner(5), 3) + unpacked(face(0), 3) + unpacked(corner(4), 3), axis=0
            )
            store_ext(xi, mid, low, high)
            return carry

        lax.fori_loop(0, SUB, fill, 0)

    def store_ext(xi, mid, low, high):
        group = lane_group(mid.shape)
        ext[SUB + xi] = mid
        ext[xi] = jnp.where(group == 0, low, pltpu.roll(mid, MAPS, 1))
        ext[2 * SUB + xi] = jnp.where(group == BLOCKS - 1, high, pltpu.roll(mid, LANES - MAPS, 1))

    def shift(sh, d):
        def body(xi, carry):
            for j in range(3):
                window = ext[xi, pl.ds(REACH + (j - 1) * d, TILE), :]
                sh[xi, :, j * LANES : (j + 1) * LANES] = window.astype(jnp.bfloat16)
            return carry

        lax.fori_loop(0, 3 * SUB, body, 0)

    def windows(sh, c, i, d):
        return sh[pl.ds(SUB + 8 * c + (i - 1) * d, 8)].reshape(8 * TILE, 3 * LANES)

    def convolved(sh, w_ref, layer, c, d):
        total = None
        for i in range(3):
            part = jnp.dot(
                windows(sh, c, i, d), w_ref[layer, i], preferred_element_type=jnp.float32
            )
            total = part if total is None else total + part
        return total

    def kernel_sums(sh, layer, d):
        for i in range(3):
            kern_ref[layer, i] = jnp.zeros((LANES, 3 * LANES), jnp.float32)

        def body(c, carry):
            left = gm_buf[rows_at(c), :]
            for i in range(3):
                kern_ref[layer, i] += lax.dot_general(
                    left,
                    windows(sh, c, i, d),
                    (((0,), (0,)), ((), ())),
                    preferred_element_type=jnp.float32,
                )
            return carry

        lax.fori_loop(0, SUB // 8, body, 0)

    def rows_at(c):
        return pl.ds(pl.multiple_of(c * 8 * TILE, 8 * TILE), 8 * TILE)

    def gather_stat(index, value):
        stat_ref[index] += jnp.sum(value.reshape(TILE, 8, LANES), axis=0)

    d0 = dil_ref[0]
    d1 = dil_ref[1]
    scale0 = par_ref[0:1, :]
    scale1 = par_ref[1:2, :]
    read = par_ref[2:3, :]
    for n in range(4):
        stat_ref[n] = jnp.zeros((8, LANES), jnp.float32)
    colg_ref[...] = jnp.zeros_like(colg_ref)

    def first(xi, carry):
        shape = (TILE + 2 * REACH, LANES)
        s = col_start - REACH + lax.broadcasted_iota(jnp.int32, shape, 0)
        group = lane_group(shape)
        window = pl.ds(SUB - 1 - xi, TILE + 2 * REACH)

        def cells(col_ref, row_ref, x, limit):
            pre = row_ref[pl.ds(xi, 1), :] + col_ref[window, :]
            inside = (s >= 0) & (s < limit) & (row_start + x - s >= 0)
            return inside, rounded(jnp.where(inside, pre * gate_of(pre), 0.0))

        inside, mid = cells(colm_ref, rowm_ref, SUB * group + xi, lim_ref[1])
        mask_buf[pl.ds(pl.multiple_of(xi * TILE, TILE), TILE), :] = inside.astype(jnp.float32)[
            REACH : REACH + TILE
        ]
        early = group < 2
        _, side = cells(
            cols_ref,
            rows_ref,
            jnp.where(early, xi - SUB, TILE + xi),
            jnp.where(early, lim_ref[0], lim_ref[2]),
        )
        store_ext(xi, mid, side, side)
        return carry

    lax.fori_loop(0, SUB, first, 0)
    shift(sh0, d0)

    def layer_first(c, carry):
        mixed = convolved(sh0, wf_ref, 0, c, d0)
        mixed_buf[rows_at(c), :] = mixed
        state = ext[pl.ds(SUB + 8 * c, 8), REACH : REACH + TILE, :].reshape(8 * TILE, LANES)
        state = mask_buf[rows_at(c), :] * (state + scale0 * (mixed * gate_of(mixed)))
        cur[pl.ds(8 * c, 8)] = rounded(state).reshape(8, TILE, LANES)
        return carry

    lax.fori_loop(0, SUB // 8, layer_first, 0)
    exchange_start(0)
    exchange_end(0)
    shift(sh1, d1)

    def layer_second(c, carry):
        mixed = convolved(sh1, wf_ref, 1, c, d1)
        gate = gate_of(mixed)
        act = mixed * gate
        mask = mask_buf[rows_at(c), :]
        state = ext[pl.ds(SUB + 8 * c, 8), REACH : REACH + TILE, :].reshape(8 * TILE, LANES)
        state = rounded(mask * (state + scale1 * act))
        terms = read * state
        high = terms.astype(jnp.bfloat16)
        low = (terms - high.astype(jnp.float32)).astype(jnp.bfloat16)
        a = lax.broadcasted_iota(jnp.int32, (LANES, LANES), 0) // MAPS
        z = lax.broadcasted_iota(jnp.int32, (LANES, LANES), 1) // MAPS
        ones = (a == z).astype(jnp.float32).astype(jnp.bfloat16)
        pred = jnp.dot(high, ones, preferred_element_type=jnp.float32) + jnp.dot(
            low, ones, preferred_element_type=jnp.float32
        )
        resid = mask * (pred - target_ref[rows_at(c), :])
        gather_stat(3, resid * resid)
        gather_stat(2, resid * state)
        adjoint = read * resid
        adj_buf[rows_at(c), :] = adjoint
        gather_stat(1, adjoint * act)
        grad = adjoint * scale1 * (gate * (1.0 + mixed * (1.0 - gate)))
        gm_buf[rows_at(c), :] = grad.astype(jnp.bfloat16)
        cur[pl.ds(8 * c, 8)] = rounded(grad).reshape(8, TILE, LANES)
        return carry

    lax.fori_loop(0, SUB // 8, layer_second, 0)
    exchange_start(1)
    kernel_sums(sh1, 1, d1)
    exchange_end(1)
    shift(sh2, d1)

    def back_second(c, carry):
        mask = mask_buf[rows_at(c), :]
        adjoint = mask * (adj_buf[rows_at(c), :] + convolved(sh2, wb_ref, 1, c, d1))
        adj_buf[rows_at(c), :] = adjoint
        mixed = mixed_buf[rows_at(c), :]
        gate = gate_of(mixed)
        gather_stat(0, adjoint * (mixed * gate))
        grad = adjoint * scale0 * (gate * (1.0 + mixed * (1.0 - gate)))
        gm_buf[rows_at(c), :] = grad.astype(jnp.bfloat16)
        cur[pl.ds(8 * c, 8)] = rounded(grad).reshape(8, TILE, LANES)
        return carry

    lax.fori_loop(0, SUB // 8, back_second, 0)
    exchange_start(2)
    kernel_sums(sh0, 0, d0)
    exchange_end(2)
    shift(sh2, d0)

    def back_first(c, carry):
        mask = mask_buf[rows_at(c), :]
        adjoint = mask * (adj_buf[rows_at(c), :] + convolved(sh2, wb_ref, 0, c, d0))
        adj_buf[rows_at(c), :] = adjoint
        return carry

    lax.fori_loop(0, SUB // 8, back_first, 0)

    def last(xi, carry):
        pre = rowm_ref[pl.ds(xi, 1), :] + colm_ref[pl.ds(SUB - 1 - xi + REACH, TILE), :]
        gate = gate_of(pre)
        grad = adj_buf[pl.ds(pl.multiple_of(xi * TILE, TILE), TILE), :]
        grad = grad * gate * (1.0 + pre * (1.0 - gate))
        rowg_ref[pl.ds(xi, 1), :] = jnp.sum(grad, axis=0, keepdims=True)
        colg_ref[pl.ds(SUB - 1 - xi, TILE), :] += grad
        return carry

    lax.fori_loop(0, SUB, last, 0)


def step_call(*args):
    nb, nd = lax.axis_size("bins"), lax.axis_size("diag")
    f32, bf16 = jnp.float32, jnp.bfloat16
    vmem = pl.BlockSpec(memory_space=pltpu.VMEM)
    smem = pl.BlockSpec(memory_space=pltpu.SMEM)
    cells = SUB * TILE
    return pl.pallas_call(
        lambda *refs: step_kernel(nb, nd, *refs),
        out_shape=(
            jax.ShapeDtypeStruct((2, 3, LANES, 3 * LANES), f32),
            jax.ShapeDtypeStruct((4, 8, LANES), f32),
            jax.ShapeDtypeStruct((SUB, LANES), f32),
            jax.ShapeDtypeStruct((SUB + TILE, LANES), f32),
        ),
        in_specs=[smem, smem] + [vmem] * 8,
        out_specs=(vmem,) * 4,
        scratch_shapes=[
            pltpu.VMEM((3 * SUB, TILE + 2 * REACH, LANES), f32),
            pltpu.VMEM((3 * SUB, TILE, 3 * LANES), bf16),
            pltpu.VMEM((3 * SUB, TILE, 3 * LANES), bf16),
            pltpu.VMEM((3 * SUB, TILE, 3 * LANES), bf16),
            pltpu.VMEM((SUB, TILE, LANES), f32),
            pltpu.VMEM((cells, LANES), f32),
            pltpu.VMEM((cells, LANES), f32),
            pltpu.VMEM((cells, LANES), f32),
            pltpu.VMEM((cells, LANES), bf16),
            pltpu.VMEM((4, FACE, LANES), bf16),
            pltpu.VMEM((4, CORNER, LANES), bf16),
            pltpu.VMEM((3, 4, FACE, LANES), bf16),
            pltpu.VMEM((3, 4, CORNER, LANES), bf16),
            pltpu.VMEM((4, CORNER, LANES), f32),
            pltpu.SemaphoreType.DMA((3, 8)),
            pltpu.SemaphoreType.DMA((3, 8)),
        ],
        compiler_params=pltpu.CompilerParams(
            collective_id=3, has_side_effects=True, vmem_limit_bytes=60 * 2**20
        ),
    )(*args)


def local(embeddings, w_row, w_col, conv_w, coef, w_out, dilation, band_tiles, bucket, target):
    rows = embeddings.shape[0]
    width = target.shape[1]
    diag_count = lax.axis_size("diag")
    total_bins = rows * lax.axis_size("bins")
    band_cols = width * diag_count
    tile_total = band_tiles.shape[0]
    zero = jnp.zeros((), jnp.int32)
    row_start = lax.axis_index("bins") * rows
    col_start = lax.axis_index("diag") * width
    device_bucket = jnp.sum(
        jnp.where(jnp.arange(diag_count, dtype=jnp.int32) == lax.axis_index("diag"), bucket, 0)
    )
    choose = (jnp.arange(BUCKETS, dtype=jnp.int32) == device_bucket).astype(jnp.float32)
    tile_ids = jnp.arange(tile_total, dtype=jnp.int32)[None, :]

    def row_limit(bins_col):
        tiles = jnp.clip(bins_col // TILE, 0, tile_total - 1)
        hits = tiles == tile_ids
        return jnp.sum(jnp.where(hits, band_tiles[None, :], 0), axis=1, keepdims=True) * TILE

    proj = jnp.dot(
        embeddings, jnp.concatenate([w_row, w_col], axis=1), preferred_element_type=jnp.float32
    ).astype(jnp.bfloat16)
    gathered = lax.all_gather(proj, "bins", axis=0, tiled=True).astype(jnp.float32)
    row_table = jnp.pad(gathered[:, :MAPS], ((REACH, REACH), (0, 0)))
    row_here = lax.dynamic_slice_in_dim(row_table, row_start, rows + 2 * REACH, 0)
    row_mid = row_here[REACH : REACH + rows].reshape(BLOCKS, SUB, MAPS)
    row_mid = row_mid.transpose(1, 0, 2).reshape(SUB, LANES)
    row_side = jnp.concatenate([row_here[:SUB]] * 2 + [row_here[REACH + rows :]] * 2, axis=1)
    front = band_cols + 2 * REACH
    col_table = jnp.pad(gathered[:, MAPS:], ((front, 4 * REACH), (0, 0)))
    col_here = lax.dynamic_slice_in_dim(
        col_table, row_start - col_start - 192 + front, 384, 0
    )[::-1]
    col_mid = jnp.concatenate([col_here[128 - SUB * q : 352 - SUB * q] for q in range(4)], axis=1)
    col_side = jnp.concatenate([col_here[160:384]] * 2 + [col_here[0:224]] * 2, axis=1)
    taps = conv_w.reshape(LAYERS, 3, 3, MAPS, MAPS)
    same = jnp.eye(BLOCKS, dtype=conv_w.dtype)

    def spread(t):
        full = t[:, :, :, None, :, None, :] * same[:, None, :, None]
        return full.reshape(LAYERS, 3, 3 * LANES, LANES)

    forward = spread(taps.transpose(0, 1, 2, 4, 3))
    backward = spread(taps[:, ::-1, ::-1])
    scales = jnp.sum(choose[None, :, None] * coef, axis=1)
    params = jnp.concatenate([scales, w_out[None], jnp.zeros((5, MAPS), jnp.float32)], axis=0)
    params = jnp.tile(params, (1, BLOCKS))
    goal = jnp.broadcast_to(
        target.reshape(BLOCKS, SUB, width).transpose(1, 2, 0)[..., None],
        (SUB, width, BLOCKS, MAPS),
    ).reshape(SUB * width, LANES)
    near = (row_start // TILE + jnp.arange(-1, 2, dtype=jnp.int32))[:, None]
    limits = jnp.sum(jnp.where(near == tile_ids, band_tiles[None, :], 0), axis=1) * TILE
    kern, stats, row_out, col_out = step_call(
        dilation, limits, col_mid, col_side, row_mid, row_side, forward, backward, params, goal
    )
    kern = kern.reshape(LAYERS, 3, BLOCKS, MAPS, 3, BLOCKS, MAPS)
    kern = sum(kern[:, :, q, :, :, q, :] for q in range(BLOCKS))
    kernels = kern.transpose(0, 1, 3, 2, 4).reshape(LAYERS, 9, MAPS, MAPS)
    stats = jnp.sum(stats, axis=1).reshape(4, BLOCKS, MAPS)
    loss_part = 0.5 * jnp.sum(stats[3, :, 0])
    stats = jnp.sum(stats, axis=1)
    out_grad = stats[2]
    coef_terms = choose[None, :, None] * stats[:2, None, :]
    row_terms = row_out.reshape(SUB, BLOCKS, MAPS).transpose(1, 0, 2).reshape(rows, MAPS)
    col_terms = sum(
        jnp.pad(
            col_out[:, q * MAPS : (q + 1) * MAPS], ((96 - SUB * q, SUB * q), (0, 0))
        )
        for q in range(BLOCKS)
    )[::-1]
    table_base = row_start - col_start - TILE + band_cols
    column_full = jnp.zeros((total_bins + band_cols, MAPS), jnp.float32)
    column_full = lax.dynamic_update_slice(column_full, col_terms, (table_base, zero))
    row_full = jnp.zeros((total_bins, MAPS), jnp.float32)
    row_full = lax.dynamic_update_slice(row_full, row_terms, (row_start, zero))
    both = jnp.concatenate([row_full, column_full[band_cols:]], axis=0).reshape(-1)
    both = all_sum(both, 1).reshape(2, total_bins, MAPS)
    row_total = lax.dynamic_slice_in_dim(both[0], row_start, rows, 0)
    column_total = lax.dynamic_slice_in_dim(both[1], row_start, rows, 0)
    row_all = row_total.astype(jnp.bfloat16)
    column_all = column_total.astype(jnp.bfloat16)
    grad_embeddings = jnp.dot(row_all, w_row.T, preferred_element_type=jnp.float32) + jnp.dot(
        column_all, w_col.T, preferred_element_type=jnp.float32
    )
    share_rows = rows // diag_count
    share_start = lax.axis_index("diag") * share_rows
    row_grad = lax.dynamic_slice_in_dim(row_all, share_start, share_rows, 0)
    col_grad = lax.dynamic_slice_in_dim(column_all, share_start, share_rows, 0)
    piece_rows = lax.dynamic_slice_in_dim(embeddings, share_start, share_rows, 0)
    row_weight = jnp.dot(piece_rows.T, row_grad, preferred_element_type=jnp.float32)
    col_weight = jnp.dot(piece_rows.T, col_grad, preferred_element_type=jnp.float32)
    pieces = (
        kernels,
        row_weight,
        col_weight,
        coef_terms,
        out_grad,
        loss_part.reshape(1),
    )
    flat = all_sum(jnp.concatenate([p.reshape(-1) for p in pieces]), 2)
    sums = []
    at = 0
    for piece in pieces:
        sums.append(flat[at : at + piece.size].reshape(piece.shape))
        at += piece.size
    totals = (sums[5][0], sums[4], sums[0], sums[3], sums[1], sums[2])
    all_bins = jnp.arange(total_bins, dtype=jnp.int32)[:, None]
    count = jnp.sum(jnp.minimum(row_limit(all_bins)[:, 0], all_bins[:, 0] + 1)).astype(jnp.float32)
    inv_root = 1.0 / jnp.sqrt(count)
    loss = jnp.reshape(totals[0] / count, (1,))
    return (
        loss,
        grad_embeddings,
        totals[2] * inv_root,
        totals[3] * inv_root,
        totals[1] * inv_root,
        totals[4] * inv_root,
        totals[5] * inv_root,
    )


def solution(mesh):
    in_specs = (P("bins", None), P(), P(), P(), P(), P(), P(), P(), P(), P("bins", "diag"))
    out_specs = (P(), P("bins", None), P(), P(), P(), P(), P())
    return jax.shard_map(local, mesh=mesh, in_specs=in_specs, out_specs=out_specs, check_vma=False)
```

```python
import jax
import jax.numpy as jnp
from jax import lax
from jax.experimental import pallas as pl
from jax.experimental.pallas import tpu as pltpu
from jax.sharding import PartitionSpec as P

MAPS = 32
TILE = 128
LAYERS = 2
REACH = 32
BUCKETS = 8


MESH = pl.DeviceIdType.MESH


def reduce_kernel(nb, nd, x_ref, o_ref, buf_a, acc_a, buf_b, acc_b, *sems):
    sa, ra, sb, rb, sc, rc, sd, rd = sems
    b = lax.axis_index("bins")
    g = lax.axis_index("diag")
    rows_a = x_ref.shape[0] // nd
    rows_b = rows_a // nb
    peers_g = [lax.rem(g + k, nd) for k in range(nd)]
    peers_b = [lax.rem(b + k, nb) for k in range(nb)]
    barrier = pltpu.get_barrier_semaphore()
    for k in range(1, nd):
        pl.semaphore_signal(barrier, inc=1, device_id=(b, peers_g[k]), device_id_type=MESH)
    for k in range(1, nb):
        pl.semaphore_signal(barrier, inc=1, device_id=(peers_b[k], g), device_id_type=MESH)
    pl.semaphore_wait(barrier, nd + nb - 2)

    def rows_of(index, count):
        return pl.ds(pl.multiple_of(index * count, 8), count)

    def send(src, dst, ssem, rsem, target):
        copy = pltpu.make_async_remote_copy(
            src_ref=src,
            dst_ref=dst,
            send_sem=ssem,
            recv_sem=rsem,
            device_id=target,
            device_id_type=MESH,
        )
        copy.start()
        return copy

    copies = [
        send(
            x_ref.at[rows_of(peers_g[k], rows_a)],
            buf_a.at[k],
            sa.at[k],
            ra.at[k],
            (b, peers_g[k]),
        )
        for k in range(1, nd)
    ]
    total = x_ref[rows_of(g, rows_a), :]
    for k in range(1, nd):
        copies[k - 1].wait()
        total = total + buf_a[k]
    acc_a[...] = total
    copies = [
        send(
            acc_a.at[rows_of(peers_b[k], rows_b)],
            buf_b.at[k],
            sb.at[k],
            rb.at[k],
            (peers_b[k], g),
        )
        for k in range(1, nb)
    ]
    total = acc_a[rows_of(b, rows_b), :]
    for k in range(1, nb):
        copies[k - 1].wait()
        total = total + buf_b[k]
    acc_b[rows_of(b, rows_b), :] = total
    mine = acc_b.at[rows_of(b, rows_b)]
    copies = [
        send(mine, mine, sc.at[k], rc.at[k], (peers_b[k], g)) for k in range(1, nb)
    ]
    for copy in copies:
        copy.wait()
    o_ref[rows_of(g, rows_a), :] = acc_b[...]
    place = o_ref.at[rows_of(g, rows_a)]
    copies = [
        send(acc_b, place, sd.at[k], rd.at[k], (b, peers_g[k])) for k in range(1, nd)
    ]
    for copy in copies:
        copy.wait()


def all_sum(flat, ident):
    nb, nd = lax.axis_size("bins"), lax.axis_size("diag")
    unit = nb * nd * 8
    rows = -(-flat.shape[0] // (128 * unit)) * unit
    x = jnp.pad(flat, (0, rows * 128 - flat.shape[0])).reshape(rows, 128)
    rows_a, rows_b = rows // nd, rows // nd // nb
    dma = pltpu.SemaphoreType.DMA
    out = pl.pallas_call(
        lambda *refs: reduce_kernel(nb, nd, *refs),
        out_shape=jax.ShapeDtypeStruct((rows, 128), jnp.float32),
        in_specs=[pl.BlockSpec(memory_space=pltpu.VMEM)],
        out_specs=pl.BlockSpec(memory_space=pltpu.VMEM),
        scratch_shapes=[
            pltpu.VMEM((nd, rows_a, 128), jnp.float32),
            pltpu.VMEM((rows_a, 128), jnp.float32),
            pltpu.VMEM((nb, rows_b, 128), jnp.float32),
            pltpu.VMEM((rows_a, 128), jnp.float32),
            dma((nd,)),
            dma((nd,)),
            dma((nb,)),
            dma((nb,)),
            dma((nb,)),
            dma((nb,)),
            dma((nd,)),
            dma((nd,)),
        ],
        compiler_params=pltpu.CompilerParams(
            collective_id=ident, has_side_effects=True, vmem_limit_bytes=16 * 2**20
        ),
    )(x)
    return out.reshape(-1)[: flat.shape[0]]


def greet(nb, nd, over_diag):
    b = lax.axis_index("bins")
    g = lax.axis_index("diag")
    barrier = pltpu.get_barrier_semaphore()
    for k in range(1, nb):
        pl.semaphore_signal(
            barrier, inc=1, device_id=(lax.rem(b + k, nb), g), device_id_type=MESH
        )
    if over_diag:
        for k in range(1, nd):
            pl.semaphore_signal(
                barrier, inc=1, device_id=(b, lax.rem(g + k, nd)), device_id_type=MESH
            )
    pl.semaphore_wait(barrier, nb - 1 + (nd - 1 if over_diag else 0))


def send_to(src, dst, ssem, rsem, target):
    copy = pltpu.make_async_remote_copy(
        src_ref=src,
        dst_ref=dst,
        send_sem=ssem,
        recv_sem=rsem,
        device_id=target,
        device_id_type=MESH,
    )
    copy.start()
    return copy


def gather_kernel(nb, nd, x_ref, o_ref, ssem, rsem):
    b = lax.axis_index("bins")
    g = lax.axis_index("diag")
    greet(nb, nd, False)
    rows = x_ref.shape[0]
    mine = pl.ds(pl.multiple_of(b * rows, rows), rows)
    copies = [
        send_to(x_ref, o_ref.at[mine], ssem.at[k], rsem.at[k], (lax.rem(b + k, nb), g))
        for k in range(1, nb)
    ]
    o_ref[mine, :] = x_ref[...]
    for copy in copies:
        copy.wait()


def gather_bins(x):
    nb, nd = lax.axis_size("bins"), lax.axis_size("diag")
    vmem = pl.BlockSpec(memory_space=pltpu.VMEM)
    return pl.pallas_call(
        lambda *refs: gather_kernel(nb, nd, *refs),
        out_shape=jax.ShapeDtypeStruct((nb * x.shape[0], x.shape[1]), x.dtype),
        in_specs=[vmem],
        out_specs=vmem,
        scratch_shapes=[pltpu.SemaphoreType.DMA((nb,)), pltpu.SemaphoreType.DMA((nb,))],
        compiler_params=pltpu.CompilerParams(
            collective_id=4, has_side_effects=True, vmem_limit_bytes=8 * 2**20
        ),
    )(x)


def owner_kernel(nb, nd, row_ref, col_ref, o_ref, buf_b, buf_g, sb, rb, sg, rg):
    b = lax.axis_index("bins")
    g = lax.axis_index("diag")
    greet(nb, nd, True)
    rows = row_ref.shape[0]

    def rows_of(index):
        return pl.ds(pl.multiple_of(index * rows, 8), rows)

    peers = [lax.rem(b + k, nb) for k in range(nb)]
    copies = [
        send_to(col_ref.at[rows_of(peers[k])], buf_b.at[k], sb.at[k], rb.at[k], (peers[k], g))
        for k in range(1, nb)
    ]
    total = col_ref[rows_of(b), :]
    for k in range(1, nb):
        copies[k - 1].wait()
        total = total + buf_b[k]
    buf_g[g, 0:rows, :] = row_ref[...]
    buf_g[g, rows : 2 * rows, :] = total
    copies = [
        send_to(buf_g.at[g], buf_g.at[g], sg.at[k], rg.at[k], (b, lax.rem(g + k, nd)))
        for k in range(1, nd)
    ]
    for copy in copies:
        copy.wait()
    total = buf_g[0]
    for k in range(1, nd):
        total = total + buf_g[k]
    o_ref[...] = total


def owner_sum(row, col):
    nb, nd = lax.axis_size("bins"), lax.axis_size("diag")
    vmem = pl.BlockSpec(memory_space=pltpu.VMEM)
    dma = pltpu.SemaphoreType.DMA
    rows = row.shape[0]
    return pl.pallas_call(
        lambda *refs: owner_kernel(nb, nd, *refs),
        out_shape=jax.ShapeDtypeStruct((2 * rows, 128), jnp.float32),
        in_specs=[vmem, vmem],
        out_specs=vmem,
        scratch_shapes=[
            pltpu.VMEM((nb, rows, 128), jnp.float32),
            pltpu.VMEM((nd, 2 * rows, 128), jnp.float32),
            dma((nb,)),
            dma((nb,)),
            dma((nd,)),
            dma((nd,)),
        ],
        compiler_params=pltpu.CompilerParams(
            collective_id=1, has_side_effects=True, vmem_limit_bytes=8 * 2**20
        ),
    )(row, col)


DIRS = [(-1, 0), (1, 0), (0, -1), (0, 1), (-1, -1), (-1, 1), (1, -1), (1, 1)]
BLOCKS = 4
SUB = 32
LANES = BLOCKS * MAPS
FACE = SUB * 32
CORNER = SUB * 8


def gate_of(v):
    return 1.0 / (1.0 + jnp.exp(-v))


def rounded(v):
    return v.astype(jnp.bfloat16).astype(jnp.float32)


def lane_group(shape):
    return lax.broadcasted_iota(jnp.int32, shape, len(shape) - 1) // MAPS


def packed(cells, group):
    piece = cells.shape[1] // BLOCKS
    total = None
    for q in range(BLOCKS):
        part = cells[:, q * piece : (q + 1) * piece, :].reshape(-1, LANES)
        turn = (MAPS * (q - group)) % LANES
        part = pltpu.roll(part, turn, 1) if turn else part
        total = part if total is None else jnp.where(lane_group(part.shape) == q, part, total)
    return total


def unpacked(part, group):
    pieces = []
    for q in range(BLOCKS):
        turn = (MAPS * (group - q)) % LANES
        pieces.append(pltpu.roll(part, turn, 1) if turn else part)
    return pieces


def step_kernel(
    nb,
    nd,
    dil_ref,
    lim_ref,
    colm_ref,
    cols_ref,
    rowm_ref,
    rows_ref,
    wf_ref,
    wb_ref,
    par_ref,
    target_ref,
    kern_ref,
    stat_ref,
    rowg_ref,
    colg_ref,
    ext,
    sh0,
    sh1,
    sh2,
    cur,
    mask_buf,
    mixed_buf,
    adj_buf,
    gm_buf,
    send_face,
    send_corner,
    recv_face,
    recv_corner,
    corner_f,
    send_sem,
    recv_sem,
):
    b = lax.axis_index("bins")
    g = lax.axis_index("diag")
    row_start = b * TILE
    col_start = g * TILE

    def there(sx, sg):
        x, y = b + sx, g + sg
        return (x >= 0) & (x < nb) & (y >= 0) & (y < nd)

    def place(sx, sg):
        return (lax.rem(b + sx + nb, nb), lax.rem(g + sg + nd, nd))

    for n, (sx, sg) in enumerate(DIRS):

        @pl.when(jnp.logical_not(there(-sx, -sg)))
        def _():
            for e in range(3):
                if n < 4:
                    recv_face[e, n] = jnp.zeros((FACE, LANES), jnp.bfloat16)
                else:
                    recv_corner[e, n - 4] = jnp.zeros((CORNER, LANES), jnp.bfloat16)

    barrier = pltpu.get_barrier_semaphore()
    for sx, sg in DIRS:

        @pl.when(there(sx, sg))
        def _():
            pl.semaphore_signal(barrier, inc=1, device_id=place(sx, sg), device_id_type=MESH)

    pl.semaphore_wait(barrier, sum(there(sx, sg).astype(jnp.int32) for sx, sg in DIRS))

    def copy_of(e, n):
        if n < 4:
            src, dst = send_face.at[n], recv_face.at[e, n]
        else:
            src, dst = send_corner.at[n - 4], recv_corner.at[e, n - 4]
        return pltpu.make_async_remote_copy(
            src_ref=src,
            dst_ref=dst,
            send_sem=send_sem.at[e, n],
            recv_sem=recv_sem.at[e, n],
            device_id=place(*DIRS[n]),
            device_id_type=MESH,
        )

    def exchange_start(e):
        for n in (2, 3, 0, 1, 4, 5, 6, 7):
            sx, sg = DIRS[n]
            lo = 0 if sg < 0 else TILE - 32
            if n < 2:
                value = packed(cur[...], 0 if sx < 0 else BLOCKS - 1)
                send_face[n] = value.astype(jnp.bfloat16)
            elif n < 4:
                value = cur[:, lo : lo + 32, :].reshape(FACE, LANES)
                send_face[n] = value.astype(jnp.bfloat16)
            else:
                value = packed(cur[:, lo : lo + 32, :], 0 if sx < 0 else BLOCKS - 1)
                send_corner[n - 4] = value.astype(jnp.bfloat16)

            @pl.when(there(sx, sg))
            def _():
                copy_of(e, n).start()

    def exchange_end(e):
        for n, (sx, sg) in enumerate(DIRS):

            @pl.when(there(-sx, -sg))
            def _():
                copy_of(e, n).wait_recv()

            @pl.when(there(sx, sg))
            def _():
                copy_of(e, n).wait_send()

        for c in range(4):
            corner_f[c] = recv_corner[e, c].astype(jnp.float32)

        def fill(xi, carry):
            face_rows = pl.ds(pl.multiple_of(xi * 32, 32), 32)
            corner_rows = pl.ds(pl.multiple_of(xi * 8, 8), 8)

            def face(n):
                return recv_face[e, n, face_rows, :].astype(jnp.float32)

            def corner(n):
                return corner_f[n - 4, corner_rows, :]

            mid = jnp.concatenate([face(3), cur[xi], face(2)], axis=0)
            low = jnp.concatenate(
                unpacked(corner(7), 0) + unpacked(face(1), 0) + unpacked(corner(6), 0), axis=0
            )
            high = jnp.concatenate(
                unpacked(corner(5), 3) + unpacked(face(0), 3) + unpacked(corner(4), 3), axis=0
            )
            store_ext(xi, mid, low, high)
            return carry

        lax.fori_loop(0, SUB, fill, 0)

    def store_ext(xi, mid, low, high):
        group = lane_group(mid.shape)
        ext[SUB + xi] = mid
        ext[xi] = jnp.where(group == 0, low, pltpu.roll(mid, MAPS, 1))
        ext[2 * SUB + xi] = jnp.where(group == BLOCKS - 1, high, pltpu.roll(mid, LANES - MAPS, 1))

    def shift(sh, d):
        def body(xi, carry):
            for j in range(3):
                window = ext[xi, pl.ds(REACH + (j - 1) * d, TILE), :]
                sh[xi, :, j * LANES : (j + 1) * LANES] = window.astype(jnp.bfloat16)
            return carry

        lax.fori_loop(0, 3 * SUB, body, 0)

    def windows(sh, c, i, d):
        return sh[pl.ds(SUB + 8 * c + (i - 1) * d, 8)].reshape(8 * TILE, 3 * LANES)

    def convolved(sh, w_ref, layer, c, d):
        total = None
        for i in range(3):
            part = jnp.dot(
                windows(sh, c, i, d), w_ref[layer, i], preferred_element_type=jnp.float32
            )
            total = part if total is None else total + part
        return total

    def kernel_sums(sh, layer, d):
        for i in range(3):
            kern_ref[layer, i] = jnp.zeros((LANES, 3 * LANES), jnp.float32)

        def body(c, carry):
            left = gm_buf[rows_at(c), :]
            for i in range(3):
                kern_ref[layer, i] += lax.dot_general(
                    left,
                    windows(sh, c, i, d),
                    (((0,), (0,)), ((), ())),
                    preferred_element_type=jnp.float32,
                )
            return carry

        lax.fori_loop(0, SUB // 8, body, 0)

    def rows_at(c):
        return pl.ds(pl.multiple_of(c * 8 * TILE, 8 * TILE), 8 * TILE)

    def gather_stat(index, value):
        stat_ref[index] += jnp.sum(value.reshape(TILE, 8, LANES), axis=0)

    d0 = dil_ref[0]
    d1 = dil_ref[1]
    scale0 = par_ref[0:1, :]
    scale1 = par_ref[1:2, :]
    read = par_ref[2:3, :]
    for n in range(4):
        stat_ref[n] = jnp.zeros((8, LANES), jnp.float32)
    colg_ref[...] = jnp.zeros_like(colg_ref)

    def first(xi, carry):
        shape = (TILE + 2 * REACH, LANES)
        s = col_start - REACH + lax.broadcasted_iota(jnp.int32, shape, 0)
        group = lane_group(shape)
        window = pl.ds(SUB - 1 - xi, TILE + 2 * REACH)

        def cells(col_ref, row_ref, x, limit):
            pre = row_ref[pl.ds(xi, 1), :] + col_ref[window, :]
            inside = (s >= 0) & (s < limit) & (row_start + x - s >= 0)
            return inside, rounded(jnp.where(inside, pre * gate_of(pre), 0.0))

        inside, mid = cells(colm_ref, rowm_ref, SUB * group + xi, lim_ref[1])
        mask_buf[pl.ds(pl.multiple_of(xi * TILE, TILE), TILE), :] = inside.astype(jnp.float32)[
            REACH : REACH + TILE
        ]
        early = group < 2
        _, side = cells(
            cols_ref,
            rows_ref,
            jnp.where(early, xi - SUB, TILE + xi),
            jnp.where(early, lim_ref[0], lim_ref[2]),
        )
        store_ext(xi, mid, side, side)
        return carry

    lax.fori_loop(0, SUB, first, 0)
    shift(sh0, d0)

    def layer_first(c, carry):
        mixed = convolved(sh0, wf_ref, 0, c, d0)
        mixed_buf[rows_at(c), :] = mixed
        state = ext[pl.ds(SUB + 8 * c, 8), REACH : REACH + TILE, :].reshape(8 * TILE, LANES)
        state = mask_buf[rows_at(c), :] * (state + scale0 * (mixed * gate_of(mixed)))
        cur[pl.ds(8 * c, 8)] = rounded(state).reshape(8, TILE, LANES)
        return carry

    lax.fori_loop(0, SUB // 8, layer_first, 0)
    exchange_start(0)
    exchange_end(0)
    shift(sh1, d1)

    def layer_second(c, carry):
        mixed = convolved(sh1, wf_ref, 1, c, d1)
        gate = gate_of(mixed)
        act = mixed * gate
        mask = mask_buf[rows_at(c), :]
        state = ext[pl.ds(SUB + 8 * c, 8), REACH : REACH + TILE, :].reshape(8 * TILE, LANES)
        state = rounded(mask * (state + scale1 * act))
        terms = read * state
        high = terms.astype(jnp.bfloat16)
        low = (terms - high.astype(jnp.float32)).astype(jnp.bfloat16)
        a = lax.broadcasted_iota(jnp.int32, (LANES, LANES), 0) // MAPS
        z = lax.broadcasted_iota(jnp.int32, (LANES, LANES), 1) // MAPS
        ones = (a == z).astype(jnp.float32).astype(jnp.bfloat16)
        pred = jnp.dot(high, ones, preferred_element_type=jnp.float32) + jnp.dot(
            low, ones, preferred_element_type=jnp.float32
        )
        resid = mask * (pred - target_ref[rows_at(c), :])
        gather_stat(3, resid * resid)
        gather_stat(2, resid * state)
        adjoint = read * resid
        adj_buf[rows_at(c), :] = adjoint
        gather_stat(1, adjoint * act)
        grad = adjoint * scale1 * (gate * (1.0 + mixed * (1.0 - gate)))
        gm_buf[rows_at(c), :] = grad.astype(jnp.bfloat16)
        cur[pl.ds(8 * c, 8)] = rounded(grad).reshape(8, TILE, LANES)
        return carry

    lax.fori_loop(0, SUB // 8, layer_second, 0)
    exchange_start(1)
    kernel_sums(sh1, 1, d1)
    exchange_end(1)
    shift(sh2, d1)

    def back_second(c, carry):
        mask = mask_buf[rows_at(c), :]
        adjoint = mask * (adj_buf[rows_at(c), :] + convolved(sh2, wb_ref, 1, c, d1))
        adj_buf[rows_at(c), :] = adjoint
        mixed = mixed_buf[rows_at(c), :]
        gate = gate_of(mixed)
        gather_stat(0, adjoint * (mixed * gate))
        grad = adjoint * scale0 * (gate * (1.0 + mixed * (1.0 - gate)))
        gm_buf[rows_at(c), :] = grad.astype(jnp.bfloat16)
        cur[pl.ds(8 * c, 8)] = rounded(grad).reshape(8, TILE, LANES)
        return carry

    lax.fori_loop(0, SUB // 8, back_second, 0)
    exchange_start(2)
    kernel_sums(sh0, 0, d0)
    exchange_end(2)
    shift(sh2, d0)

    def back_first(c, carry):
        mask = mask_buf[rows_at(c), :]
        adjoint = mask * (adj_buf[rows_at(c), :] + convolved(sh2, wb_ref, 0, c, d0))
        adj_buf[rows_at(c), :] = adjoint
        return carry

    lax.fori_loop(0, SUB // 8, back_first, 0)

    def last(xi, carry):
        pre = rowm_ref[pl.ds(xi, 1), :] + colm_ref[pl.ds(SUB - 1 - xi + REACH, TILE), :]
        gate = gate_of(pre)
        grad = adj_buf[pl.ds(pl.multiple_of(xi * TILE, TILE), TILE), :]
        grad = grad * gate * (1.0 + pre * (1.0 - gate))
        rowg_ref[pl.ds(xi, 1), :] = jnp.sum(grad, axis=0, keepdims=True)
        colg_ref[pl.ds(SUB - 1 - xi, TILE), :] += grad
        return carry

    lax.fori_loop(0, SUB, last, 0)


def step_call(*args):
    nb, nd = lax.axis_size("bins"), lax.axis_size("diag")
    f32, bf16 = jnp.float32, jnp.bfloat16
    vmem = pl.BlockSpec(memory_space=pltpu.VMEM)
    smem = pl.BlockSpec(memory_space=pltpu.SMEM)
    cells = SUB * TILE
    return pl.pallas_call(
        lambda *refs: step_kernel(nb, nd, *refs),
        out_shape=(
            jax.ShapeDtypeStruct((2, 3, LANES, 3 * LANES), f32),
            jax.ShapeDtypeStruct((4, 8, LANES), f32),
            jax.ShapeDtypeStruct((SUB, LANES), f32),
            jax.ShapeDtypeStruct((SUB + TILE, LANES), f32),
        ),
        in_specs=[smem, smem] + [vmem] * 8,
        out_specs=(vmem,) * 4,
        scratch_shapes=[
            pltpu.VMEM((3 * SUB, TILE + 2 * REACH, LANES), f32),
            pltpu.VMEM((3 * SUB, TILE, 3 * LANES), bf16),
            pltpu.VMEM((3 * SUB, TILE, 3 * LANES), bf16),
            pltpu.VMEM((3 * SUB, TILE, 3 * LANES), bf16),
            pltpu.VMEM((SUB, TILE, LANES), f32),
            pltpu.VMEM((cells, LANES), f32),
            pltpu.VMEM((cells, LANES), f32),
            pltpu.VMEM((cells, LANES), f32),
            pltpu.VMEM((cells, LANES), bf16),
            pltpu.VMEM((4, FACE, LANES), bf16),
            pltpu.VMEM((4, CORNER, LANES), bf16),
            pltpu.VMEM((3, 4, FACE, LANES), bf16),
            pltpu.VMEM((3, 4, CORNER, LANES), bf16),
            pltpu.VMEM((4, CORNER, LANES), f32),
            pltpu.SemaphoreType.DMA((3, 8)),
            pltpu.SemaphoreType.DMA((3, 8)),
        ],
        compiler_params=pltpu.CompilerParams(
            collective_id=3, has_side_effects=True, vmem_limit_bytes=60 * 2**20
        ),
    )(*args)


def local(embeddings, w_row, w_col, conv_w, coef, w_out, dilation, band_tiles, bucket, target):
    rows = embeddings.shape[0]
    width = target.shape[1]
    diag_count = lax.axis_size("diag")
    total_bins = rows * lax.axis_size("bins")
    band_cols = width * diag_count
    tile_total = band_tiles.shape[0]
    zero = jnp.zeros((), jnp.int32)
    row_start = lax.axis_index("bins") * rows
    col_start = lax.axis_index("diag") * width
    device_bucket = jnp.sum(
        jnp.where(jnp.arange(diag_count, dtype=jnp.int32) == lax.axis_index("diag"), bucket, 0)
    )
    choose = (jnp.arange(BUCKETS, dtype=jnp.int32) == device_bucket).astype(jnp.float32)
    tile_ids = jnp.arange(tile_total, dtype=jnp.int32)[None, :]

    def row_limit(bins_col):
        tiles = jnp.clip(bins_col // TILE, 0, tile_total - 1)
        hits = tiles == tile_ids
        return jnp.sum(jnp.where(hits, band_tiles[None, :], 0), axis=1, keepdims=True) * TILE

    proj = jnp.dot(
        embeddings,
        jnp.pad(jnp.concatenate([w_row, w_col], axis=1), ((0, 0), (0, LANES - 2 * MAPS))),
        preferred_element_type=jnp.float32
    ).astype(jnp.bfloat16)
    gathered = gather_bins(proj).astype(jnp.float32)
    row_table = jnp.pad(gathered[:, :MAPS], ((REACH, REACH), (0, 0)))
    row_here = lax.dynamic_slice_in_dim(row_table, row_start, rows + 2 * REACH, 0)
    row_mid = row_here[REACH : REACH + rows].reshape(BLOCKS, SUB, MAPS)
    row_mid = row_mid.transpose(1, 0, 2).reshape(SUB, LANES)
    row_side = jnp.concatenate([row_here[:SUB]] * 2 + [row_here[REACH + rows :]] * 2, axis=1)
    front = band_cols + 2 * REACH
    col_table = jnp.pad(gathered[:, MAPS : 2 * MAPS], ((front, 4 * REACH), (0, 0)))
    col_here = lax.dynamic_slice_in_dim(
        col_table, row_start - col_start - 192 + front, 384, 0
    )[::-1]
    col_mid = jnp.concatenate([col_here[128 - SUB * q : 352 - SUB * q] for q in range(4)], axis=1)
    col_side = jnp.concatenate([col_here[160:384]] * 2 + [col_here[0:224]] * 2, axis=1)
    taps = conv_w.reshape(LAYERS, 3, 3, MAPS, MAPS)
    same = jnp.eye(BLOCKS, dtype=conv_w.dtype)

    def spread(t):
        full = t[:, :, :, None, :, None, :] * same[:, None, :, None]
        return full.reshape(LAYERS, 3, 3 * LANES, LANES)

    forward = spread(taps.transpose(0, 1, 2, 4, 3))
    backward = spread(taps[:, ::-1, ::-1])
    scales = jnp.sum(choose[None, :, None] * coef, axis=1)
    params = jnp.concatenate([scales, w_out[None], jnp.zeros((5, MAPS), jnp.float32)], axis=0)
    params = jnp.tile(params, (1, BLOCKS))
    goal = jnp.broadcast_to(
        target.reshape(BLOCKS, SUB, width).transpose(1, 2, 0)[..., None],
        (SUB, width, BLOCKS, MAPS),
    ).reshape(SUB * width, LANES)
    near = (row_start // TILE + jnp.arange(-1, 2, dtype=jnp.int32))[:, None]
    limits = jnp.sum(jnp.where(near == tile_ids, band_tiles[None, :], 0), axis=1) * TILE
    kern, stats, row_out, col_out = step_call(
        dilation, limits, col_mid, col_side, row_mid, row_side, forward, backward, params, goal
    )
    kern = kern.reshape(LAYERS, 3, BLOCKS, MAPS, 3, BLOCKS, MAPS)
    kern = sum(kern[:, :, q, :, :, q, :] for q in range(BLOCKS))
    kernels = kern.transpose(0, 1, 3, 2, 4).reshape(LAYERS, 9, MAPS, MAPS)
    stats = jnp.sum(stats, axis=1).reshape(4, BLOCKS, MAPS)
    loss_part = 0.5 * jnp.sum(stats[3, :, 0])
    stats = jnp.sum(stats, axis=1)
    out_grad = stats[2]
    coef_terms = choose[None, :, None] * stats[:2, None, :]
    row_terms = row_out.reshape(SUB, BLOCKS, MAPS).transpose(1, 0, 2).reshape(rows, MAPS)
    col_terms = sum(
        jnp.pad(
            col_out[:, q * MAPS : (q + 1) * MAPS], ((96 - SUB * q, SUB * q), (0, 0))
        )
        for q in range(BLOCKS)
    )[::-1]
    table_base = row_start - col_start - TILE + band_cols
    column_full = jnp.zeros((total_bins + band_cols, MAPS), jnp.float32)
    column_full = lax.dynamic_update_slice(column_full, col_terms, (table_base, zero))
    both = owner_sum(row_terms.reshape(-1, 128), column_full[band_cols:].reshape(-1, 128))
    row_total, column_total = both.reshape(2, rows, MAPS)
    row_all = row_total.astype(jnp.bfloat16)
    column_all = column_total.astype(jnp.bfloat16)
    grad_embeddings = jnp.dot(row_all, w_row.T, preferred_element_type=jnp.float32) + jnp.dot(
        column_all, w_col.T, preferred_element_type=jnp.float32
    )
    share_rows = rows // diag_count
    share_start = lax.axis_index("diag") * share_rows
    row_grad = lax.dynamic_slice_in_dim(row_all, share_start, share_rows, 0)
    col_grad = lax.dynamic_slice_in_dim(column_all, share_start, share_rows, 0)
    piece_rows = lax.dynamic_slice_in_dim(embeddings, share_start, share_rows, 0)
    row_weight = jnp.dot(piece_rows.T, row_grad, preferred_element_type=jnp.float32)
    col_weight = jnp.dot(piece_rows.T, col_grad, preferred_element_type=jnp.float32)
    pieces = (
        kernels,
        row_weight,
        col_weight,
        coef_terms,
        out_grad,
        loss_part.reshape(1),
    )
    flat = all_sum(jnp.concatenate([p.reshape(-1) for p in pieces]), 2)
    sums = []
    at = 0
    for piece in pieces:
        sums.append(flat[at : at + piece.size].reshape(piece.shape))
        at += piece.size
    totals = (sums[5][0], sums[4], sums[0], sums[3], sums[1], sums[2])
    all_bins = jnp.arange(total_bins, dtype=jnp.int32)[:, None]
    count = jnp.sum(jnp.minimum(row_limit(all_bins)[:, 0], all_bins[:, 0] + 1)).astype(jnp.float32)
    inv_root = 1.0 / jnp.sqrt(count)
    loss = jnp.reshape(totals[0] / count, (1,))
    return (
        loss,
        grad_embeddings,
        totals[2] * inv_root,
        totals[3] * inv_root,
        totals[1] * inv_root,
        totals[4] * inv_root,
        totals[5] * inv_root,
    )


def solution(mesh):
    in_specs = (P("bins", None), P(), P(), P(), P(), P(), P(), P(), P(), P("bins", "diag"))
    out_specs = (P(), P("bins", None), P(), P(), P(), P(), P())
    return jax.shard_map(local, mesh=mesh, in_specs=in_specs, out_specs=out_specs, check_vma=False)
```
